32 devices in a mesh: sx: 2 (over y), sy: 4 (over x, core), sz: 4 (over z).
Axes of the slice: x: 2, y: 2, z: 4, core: 2. Of those that a mesh axis runs over, the one named last changes fastest.
Arguments:
- right_side: bfloat16 [2, 4, 4, 1536, 256], P('sx', 'sy', 'sz'), may hold values from -6 to 6
- interface_inverse: bfloat16 [2, 4, 4, 1536, 1536], P('sx', 'sy', 'sz'), may hold values from -2 to 2, as said below
- face_link: int32 [2, 4, 4, 4], P('sx', 'sy', 'sz'), may hold values 0 or 1
- far_target: int32 [2, 4, 4, 8, 1], P('sx', 'sy', 'sz'), may hold values from 0 to 7; in each aligned block of 8 rows (0 to 7, 8 to 15, ..., all dimensions but the last counted through in order) at most 3 rows name the same one
- far_rank: int32 [2, 4, 4, 8], P('sx', 'sy', 'sz'), may hold values from 1 to 16
- far_basis: bfloat16 [2, 4, 4, 8, 16, 1536], P('sx', 'sy', 'sz'), may hold values from -0.15625 to 0.15625
- patch_basis: bfloat16 [2, 4, 4, 16, 1536], P('sx', 'sy', 'sz'), may hold values from -0.5 to 0.5
- corner_basis: bfloat16 [2, 4, 4, 8, 1536], P('sx', 'sy', 'sz'), may hold values from -1 to 1
- corner_row: int32 [2, 4, 4, 8], P('sx', 'sy', 'sz'), may hold values from 0 to 255
- coarse_inverse: bfloat16 [256, 256], P('sy'), may hold values from -2 to 2, as said below
Outputs:
- multipliers: float32 [2, 4, 4, 1536, 256], P('sx', 'sy', 'sz')
- interface_field: bfloat16 [2, 4, 4, 1536, 256], P('sx', 'sy', 'sz')
The draws below stay inside these ranges and needn't reach their ends.
Inputs may be any that keep to these rules, and one draw needn't show every extreme that they name: `far_target`: within one subdomain's 8 entries no target is named more than 3 times, a bound that some block reaches. `interface_inverse`: each subdomain's block is a dense matrix with a positive diagonal that exceeds its row's off-diagonal magnitude in the root-mean-square sense. `coarse_inverse`: A dense matrix with a positive diagonal that exceeds its row's off-diagonal magnitude in the root-mean-square sense.
All inputs are finite; a program needn't handle non-finite values. No bound on the sum of `face_link` on one device may be relied on, other than what follows from the above.
Results may differ from the reference program's by a relative error of at most 0.0085.
Values may be sent and summed in bfloat16 or wider, within the bound.
A program may use at most 64 MiB of HBM per device.

```python
import math
import jax
import jax.numpy as jnp
import numpy as np
from jax import lax

IF = 1536
NRHS = 256
RMAX = 16
CORNERS = 8
MOST = 3
ITERS = 2
GROUP = 8
FAR = 8
NC = 256
N_SX = 2
N_SY = 4
N_SZ = 4


def draw_interface_inverse(key, part):
    noise_key = jax.random.fold_in(key, 11)
    diagonal_key = jax.random.fold_in(key, 12)
    shape = (N_SX, N_SY, N_SZ, IF, IF)
    noise = jax.random.truncated_normal(noise_key, -4.0, 4.0, shape, jnp.float32)
    diagonal = jax.random.uniform(diagonal_key, (N_SX, N_SY, N_SZ, IF), jnp.float32, 0.3, 0.9)
    scaled = noise * (0.4 / jnp.sqrt(jnp.float32(IF)))
    return (scaled + diagonal[..., None] * jnp.eye(IF, dtype=jnp.float32)).astype(jnp.bfloat16)


def draw_coarse_inverse(key, part):
    noise_key = jax.random.fold_in(key, 21)
    diagonal_key = jax.random.fold_in(key, 22)
    noise = jax.random.truncated_normal(noise_key, -4.0, 4.0, (NC, NC), jnp.float32)
    diagonal = jax.random.uniform(diagonal_key, (NC,), jnp.float32, 0.3, 0.9)
    scaled = noise * (0.4 / jnp.sqrt(jnp.float32(NC)))
    return (scaled + diagonal[:, None] * jnp.eye(NC, dtype=jnp.float32)).astype(jnp.bfloat16)


def plant(values, rng, low, largest):
    longest = values.shape.index(max(values.shape))
    spots = []
    for shift in (0, 1):
        where = [jax.random.randint(jax.random.fold_in(rng, axis), (), 0, length) for axis, length in enumerate(values.shape)]
        where[longest] = (where[longest] + shift) % values.shape[longest]
        spots.append(tuple(where))
    return values.at[spots[0]].set(low).at[spots[1]].set(largest)


def shard_levels(own_key, shape, cuts, smallest, high):
    factor_of = 1.0
    for position, shards_of in cuts:
        draws = jax.random.uniform(jax.random.fold_in(jax.random.fold_in(own_key, 6), position), (shards_of,), jnp.float32, smallest / len(cuts), high / len(cuts))
        factor_of = factor_of * jnp.repeat(jnp.exp(draws), shape[position] // shards_of).reshape((-1,) + (1,) * (len(shape) - 1 - position))
    return factor_of


def shared_out(own_key, own, number, rows, number_of, top, most, lean):
    ranking = jax.random.permutation(own_key, number_of)
    heavy_load, common = portions_of(number_of, rows * top, most, lean, True), portions_of(number_of, rows * top, most, lean, False)
    places = jnp.arange(number_of)

    def named(sizes, turn):
        used = int((sizes > 0).sum())
        fixed = max(1, used // 4)
        shifted = fixed + (places - fixed + turn * (used - fixed)) % max(1, number_of - fixed)
        return jnp.zeros((number_of,), jnp.int32).at[ranking[jnp.where(places < fixed, places, shifted)]].set(jnp.asarray(sizes, jnp.int32))

    sizes = jnp.where(number % 4 == 0, named(heavy_load, number // 4), named(common, number - number // 4 - 1))
    mixed = jax.random.permutation(jax.random.fold_in(own, 3), number_of)
    donor, receiver = mixed[0:number_of // 2 * 2:2], mixed[1:number_of // 2 * 2:2]
    slack = jnp.minimum(sizes[donor] - 1, most - sizes[receiver]) // 2
    slack = jnp.where((donor == ranking[0]) | (receiver == ranking[0]) | (sizes[receiver] == 0), 0, jnp.maximum(slack, 0))
    shifted = jax.random.randint(jax.random.fold_in(own, 4), (number_of // 2,), 0, 1 << 20) % (slack + 1)
    sizes = sizes.at[donor].add(-shifted).at[receiver].add(shifted)
    members = jnp.searchsorted(jnp.cumsum(sizes), jnp.arange(rows * top), side="right").astype(jnp.int32)
    grid = members.reshape(top, rows).T
    grid = grid[jax.random.permutation(jax.random.fold_in(own, 1), rows)]
    turn = jax.random.randint(jax.random.fold_in(own, 2), (rows, 1), 0, top)
    return jnp.take_along_axis(grid, (jnp.arange(top)[None, :] + turn) % top, axis=1)


def portions_of(number_of, total, bound, slope, full):
    weights = [(1 << 20) // math.isqrt(rank ** slope) + 1 for rank in range(1, number_of + 1)]
    largest = bound if full else min(bound, max(-(-total // number_of), total * weights[0] // sum(weights)))
    least = 1 if total - largest >= number_of - 1 else 0
    given, spare = [largest] + [least] * (number_of - 1), total - largest - least * (number_of - 1)
    while spare > 0:
        candidates = [i for i in range(1, number_of) if given[i] < largest] or [i for i in range(1, number_of) if given[i] < bound]
        whole, budget = sum([weights[i] for i in candidates]), spare
        for i in candidates:
            more = min(bound - given[i], max(1, budget * weights[i] // whole), spare)
            given[i] = given[i] + more
            spare = spare - more
    return np.array(given)


def gaussian(own_key, dims, deviation, reach, shards=(), kind=jnp.bfloat16):
    values = deviation * jax.random.normal(own_key, dims, jnp.float32)
    if shards:
        values = values * shard_levels(own_key, dims, shards, -0.22, 0.18)
    return jnp.clip(values, -reach, reach).astype(kind)


def setup_inputs(seed: int = 0) -> dict:
    keys = jax.random.split(jax.random.key(seed), 11)
    right_side = gaussian(keys[0], (N_SX, N_SY, N_SZ, IF, NRHS), 1.0, 6.0, ((0, 2), (1, 4), (2, 4)))
    interface_inverse = draw_interface_inverse(jax.random.fold_in(keys[10], 71), 0)
    face_link = plant((jax.random.randint(keys[2], (N_SX, N_SY, N_SZ, 4), 0, 4) < 3).astype(jnp.int32), jax.random.fold_in(keys[2], 1), 0, 1)
    far_target_keys = jax.random.split(jax.random.fold_in(keys[3], 1), N_SX * N_SY * N_SZ * FAR // FAR)
    far_target_turns = jax.random.permutation(jax.random.fold_in(keys[3], 3), N_SX * N_SY * N_SZ * FAR // FAR)
    far_target = jax.vmap(lambda own, number: shared_out(jax.random.fold_in(keys[3], 2), own, number, FAR, GROUP, 1, MOST, 2))(far_target_keys, far_target_turns).reshape((N_SX, N_SY, N_SZ, FAR, 1))
    far_rank = plant(jax.random.randint(keys[4], (N_SX, N_SY, N_SZ, FAR), 1, RMAX + 1), jax.random.fold_in(keys[4], 1), 1, RMAX).astype(jnp.int32)
    far_basis = gaussian(keys[5], (N_SX, N_SY, N_SZ, FAR, RMAX, IF), IF ** -0.5, 0.15625, ((0, 2), (1, 4), (2, 4)))
    patch_basis = gaussian(keys[6], (N_SX, N_SY, N_SZ, RMAX, IF), (RMAX * FAR) ** -0.5, 0.5, ((0, 2), (1, 4), (2, 4)))
    corner_basis = gaussian(keys[7], (N_SX, N_SY, N_SZ, CORNERS, IF), 0.16, 1.0, ((0, 2), (1, 4), (2, 4)))
    corner_row = plant(jax.random.randint(keys[8], (N_SX, N_SY, N_SZ, CORNERS), 0, NC), jax.random.fold_in(keys[8], 1), 0, NC - 1).astype(jnp.int32)
    coarse_inverse = draw_coarse_inverse(jax.random.fold_in(keys[10], 71), 0)
    return dict(right_side=right_side, interface_inverse=interface_inverse, face_link=face_link, far_target=far_target, far_rank=far_rank, far_basis=far_basis, patch_basis=patch_basis, corner_basis=corner_basis, corner_row=corner_row, coarse_inverse=coarse_inverse)


def solve_each(interface_inverse, multipliers):
    order_size = interface_inverse.shape[-1]
    flat_inverse = interface_inverse.reshape(-1, order_size, order_size)
    flat_values = multipliers.astype(jnp.bfloat16).reshape((-1,) + multipliers.shape[-2:])

    def solve_one(pair):
        return jnp.dot(pair[0].astype(jnp.float32), pair[1].astype(jnp.float32), preferred_element_type=jnp.float32).astype(jnp.bfloat16)

    return lax.map(solve_one, (flat_inverse, flat_values)).reshape(multipliers.shape)


def far_coefficients(far_basis, solved, far_rank):
    flat_basis = far_basis.reshape((-1,) + far_basis.shape[-3:])
    flat_solved = solved.reshape((-1,) + solved.shape[-2:])
    flat_rank = far_rank.reshape(-1, far_rank.shape[-1])

    def coefficient_one(triple):
        basis, values, ranks = triple
        product = jnp.einsum('eri,in->ern', basis.astype(jnp.float32), values.astype(jnp.float32))
        kept = (jnp.arange(basis.shape[1], dtype=jnp.int32)[None, :] < ranks[:, None]).astype(jnp.float32)
        return (product * kept[:, :, None]).astype(jnp.bfloat16)

    result = lax.map(coefficient_one, (flat_basis, flat_solved, flat_rank))
    return result.reshape(far_basis.shape[:4] + (far_basis.shape[4], solved.shape[-1]))


def neighbour_faces(solved, face_link):
    face_rows = IF // 6
    values = solved.astype(jnp.float32)
    links = face_link.astype(jnp.float32)
    face_zero = values[..., 0:face_rows, :]
    face_one = values[..., face_rows:2 * face_rows, :]
    face_two = values[..., 2 * face_rows:3 * face_rows, :]
    face_three = values[..., 3 * face_rows:4 * face_rows, :]
    from_lower_x = jnp.concatenate([jnp.zeros_like(face_one[:1]), face_one[:-1]], axis=0)
    from_upper_x = jnp.concatenate([face_zero[1:], jnp.zeros_like(face_zero[:1])], axis=0)
    from_lower_y = jnp.concatenate([jnp.zeros_like(face_three[:, :1]), face_three[:, :-1]], axis=1)
    from_upper_y = jnp.concatenate([face_two[:, 1:], jnp.zeros_like(face_two[:, :1])], axis=1)
    rest = jnp.zeros(values.shape[:-2] + (IF - 4 * face_rows, values.shape[-1]), jnp.float32)
    return jnp.concatenate([
        links[..., 0, None, None] * from_lower_x,
        links[..., 1, None, None] * from_upper_x,
        links[..., 2, None, None] * from_lower_y,
        links[..., 3, None, None] * from_upper_y,
        rest], axis=-2)


def reference(right_side, interface_inverse, face_link, far_target, far_rank, far_basis, patch_basis, corner_basis, corner_row, coarse_inverse):
    source = right_side.astype(jnp.float32)
    multipliers = source
    target_hot = (far_target[..., 0][..., None] == jnp.arange(GROUP, dtype=jnp.int32)).astype(jnp.float32)
    for sweep in range(ITERS):
        solved = solve_each(interface_inverse, multipliers)
        neighbour = neighbour_faces(solved, face_link)
        coefficient = far_coefficients(far_basis, solved, far_rank)
        arrived = jnp.einsum('xyzeg,xyzern->ygrn', target_hot, coefficient.astype(jnp.float32))
        arrived = arrived.reshape(N_SY, N_SX, N_SZ, RMAX, NRHS).transpose(1, 0, 2, 3, 4)
        arrived_rounded = arrived.astype(jnp.bfloat16)
        far_term = jnp.einsum('xyzri,xyzrn->xyzin', patch_basis.astype(jnp.float32), arrived_rounded.astype(jnp.float32))
        corner_terms = jnp.einsum('xyzci,xyzin->xyzcn', corner_basis.astype(jnp.float32), solved.astype(jnp.float32))
        coarse_sum = jax.ops.segment_sum(corner_terms.reshape(-1, NRHS), corner_row.reshape(-1), num_segments=NC).astype(jnp.bfloat16)
        coarse_field = jnp.dot(coarse_inverse, coarse_sum, preferred_element_type=jnp.float32).astype(jnp.bfloat16)
        picked = coarse_field[corner_row]
        correction = jnp.einsum('xyzci,xyzcn->xyzin', corner_basis.astype(jnp.float32), picked.astype(jnp.float32))
        multipliers = multipliers + source - (solved.astype(jnp.float32) - neighbour) - far_term - correction
    interface_field = solve_each(interface_inverse, multipliers)
    return multipliers, interface_field
```

```python
import functools

import jax
import jax.numpy as jnp
from jax import lax
from jax.experimental import pallas as pl
from jax.experimental.pallas import tpu as pltpu
from jax.sharding import PartitionSpec as P

ITERS = 2
F32 = jnp.float32
BF16 = jnp.bfloat16
MESH = pl.DeviceIdType.MESH


def each(count, step):
    if count <= 16:
        for number in range(count):
            step(number)
    else:

        @pl.loop(0, count)
        def _(number):
            step(number)


def kernel(
    sizes,
    link,
    target,
    rank,
    corner,
    right_hbm,
    inverse_hbm,
    bases_hbm,
    patch_hbm,
    corners_hbm,
    coarse_hbm,
    out_hbm,
    field_hbm,
    right,
    inverse,
    bases,
    patch,
    corners,
    coarse,
    stacked,
    lifted,
    hot,
    mixing,
    rounded,
    solved,
    base,
    face_in,
    tx,
    rx,
    gathered,
    joint,
    final,
    field,
    load_sem,
    store_sem,
    hot_sem,
    coarse_sem,
    face_sem,
    group_sem,
    line_sem,
):
    nx, ny, nz = sizes
    group = nx * nz
    order, columns = right.shape
    face = order // 6
    entries = target.shape[0]
    limit = bases.shape[0] // entries
    count = corner.shape[0]
    twice = 2 * count
    half = columns // 2
    width = coarse.shape[-1]
    i, j, k = (lax.axis_index(name) for name in ("sx", "sy", "sz"))
    me = i * nz + k

    def member(step):
        other = lax.rem(me + 1 + step, group)
        return other // nz, lax.rem(other, nz)

    def in_line(step):
        return lax.rem(j + 1 + step, ny)

    loads = []

    def load(source, place):
        copy = pltpu.make_async_copy(source, place, load_sem.at[len(loads)])
        copy.start()
        loads.append(copy)
        return copy

    load_right = load(right_hbm, right)
    load_rows = [
        load(inverse_hbm.at[pl.ds(f * face, face)], inverse.at[pl.ds(f * face, face)])
        for f in range(6)
    ]
    load_bases = load(bases_hbm, bases)
    load_patch = load(patch_hbm, patch)
    load_corners = load(corners_hbm, corners)
    load_coarse = load(coarse_hbm, coarse.at[j])

    barrier = pltpu.get_barrier_semaphore()

    def greet(step):
        a, c = member(step)
        pl.semaphore_signal(barrier, inc=1, device_id=(a, j, c), device_id_type=MESH)

    def greet_line(step):
        pl.semaphore_signal(barrier, inc=1, device_id=(i, in_line(step), k), device_id_type=MESH)

    each(group - 1, greet)
    each(ny - 1, greet_line)

    row = lax.broadcasted_iota(jnp.int32, (twice, width), 0)
    ids = jnp.zeros((twice, width), jnp.int32)
    for q in range(count):
        ids = jnp.where(lax.rem(row, count) == q, corner[q], ids)
    lane = lax.broadcasted_iota(jnp.int32, (twice, width), 1)
    hot[j, pl.ds(pl.multiple_of(me * twice, twice), twice), :] = jnp.where(
        ids == lane, 1.0, 0.0
    ).astype(BF16)

    for number, axis_index, edge in ((0, i, 0), (1, i, nx - 1), (2, j, 0), (3, j, ny - 1)):

        @pl.when(axis_index == edge)
        def _():
            for sweep in range(ITERS):
                face_in[sweep, number] = jnp.zeros((face, columns), BF16)

    pl.semaphore_wait(barrier, group - 1 + ny - 1)

    own_hot = hot.at[j, pl.ds(pl.multiple_of(me * twice, twice), twice)]

    def send_hot(step):
        a, c = member(step)
        pltpu.make_async_remote_copy(
            own_hot, own_hot, hot_sem.at[0], hot_sem.at[1], device_id=(a, j, c), device_id_type=MESH
        ).start()

    each(group - 1, send_hot)
    load_coarse.wait()

    def send_coarse(step):
        pltpu.make_async_remote_copy(
            coarse.at[j],
            coarse.at[j],
            coarse_sem.at[0],
            coarse_sem.at[1],
            device_id=(i, in_line(step), k),
            device_id_type=MESH,
        ).start()

    each(ny - 1, send_coarse)

    load_bases.wait()
    load_patch.wait()
    load_corners.wait()
    total = entries * limit
    block = min(group * limit, 128)
    lanes = lax.broadcasted_iota(jnp.int32, (1, total), 1)
    entry = lanes // limit
    named = jnp.zeros((1, total), jnp.int32)
    kept = jnp.zeros((1, total), jnp.int32)
    for e in range(entries):
        named = jnp.where(entry == e, target[e], named)
        kept = jnp.where(entry == e, rank[e], kept)
    place = lax.rem(lanes, limit)
    wanted = jnp.where(place < kept, named * limit + place, -1)
    for start in range(0, group * limit, block):
        rows = lax.broadcasted_iota(jnp.int32, (block, total), 0) + start
        route = jnp.where(rows == wanted, 1.0, 0.0).astype(BF16)
        stacked[pl.ds(start, block), :] = jnp.dot(
            route, bases[...], preferred_element_type=F32
        ).astype(BF16)
    padded = jnp.concatenate(
        [corners[...].astype(F32), jnp.zeros((twice - count, order), F32)], axis=0
    )
    stacked[pl.ds(group * limit, twice), :] = padded.astype(BF16)
    lifted[...] = jnp.transpose(
        jnp.concatenate([patch[...].astype(F32), padded], axis=0)
    ).astype(BF16)

    load_right.wait()
    rounded[...] = right[...]

    def face_copy(sweep, f):
        if f < 2:
            to = (i + (1 if f == 1 else -1), j, k)
        else:
            to = (i, j + (1 if f == 3 else -1), k)
        return pltpu.make_async_remote_copy(
            solved.at[sweep, pl.ds(f * face, face)],
            face_in.at[sweep, f ^ 1],
            face_sem.at[sweep, f, 0],
            face_sem.at[sweep, f ^ 1, 1],
            device_id=to,
            device_id_type=MESH,
        )

    def await_face(sweep, f):
        to = ((i - 1, j, k), (i + 1, j, k), (i, j - 1, k), (i, j + 1, k))[f]
        pltpu.make_async_remote_copy(
            solved.at[sweep, pl.ds((f ^ 1) * face, face)],
            face_in.at[sweep, f],
            face_sem.at[sweep, f ^ 1, 0],
            face_sem.at[sweep, f, 1],
            device_id=to,
            device_id_type=MESH,
        ).wait_recv()

    def has(f):
        return (i > 0, i < nx - 1, j > 0, j < ny - 1)[f]

    def send_face(sweep, f):
        @pl.when(has(f))
        def _():
            face_copy(sweep, f).start()

    for sweep in range(ITERS):
        for f in range(6):
            if sweep == 0:
                load_rows[f].wait()
            part = pl.ds(f * face, face)
            product = jnp.dot(
                inverse[part, :], rounded[...], preferred_element_type=F32
            ).astype(BF16)
            solved[sweep, part, :] = product
            if f < 4:
                send_face(sweep, f)

        coefficient = jnp.dot(stacked[...], solved[sweep], preferred_element_type=F32)
        terms = coefficient[group * limit : group * limit + count]
        terms = jnp.concatenate([terms[:, :half], terms[:, half:]], axis=0).astype(BF16)
        for t in range(group):
            own = coefficient[t * limit : (t + 1) * limit].astype(BF16)
            tx[sweep, t, 0:limit, :] = own[:, :half]
            tx[sweep, t, limit : 2 * limit, :] = own[:, half:]
            tx[sweep, t, 2 * limit :, :] = terms

        def send_group(step):
            a, c = member(step)
            pltpu.make_async_remote_copy(
                tx.at[sweep, a * nz + c],
                rx.at[sweep, me],
                group_sem.at[sweep, 0],
                group_sem.at[sweep, 1],
                device_id=(a, j, c),
                device_id_type=MESH,
            ).start()

        each(group - 1, send_group)
        rx[sweep, me] = tx[sweep, me]

        if sweep == 0:
            every = hot.at[j, pl.ds(0, (group - 1) * twice)]
            pltpu.make_async_remote_copy(
                every, every, hot_sem.at[0], hot_sem.at[1], device_id=(i, in_line(0), k),
                device_id_type=MESH,
            ).wait()

            def send_hot_line(step):
                pltpu.make_async_remote_copy(
                    hot.at[j], hot.at[j], hot_sem.at[2], hot_sem.at[3],
                    device_id=(i, in_line(step), k), device_id_type=MESH,
                ).start()

            each(ny - 1, send_hot_line)

        for f in range(6):
            part = pl.ds(f * face, face)
            value = solved[sweep, part, :].astype(F32)
            source = right[part, :].astype(F32)
            before = source if sweep == 0 else final[part, :]
            base[part, :] = before + source - value

        everyone = pltpu.make_async_remote_copy(
            tx.at[sweep, pl.ds(0, group - 1)],
            rx.at[sweep, pl.ds(0, group - 1)],
            group_sem.at[sweep, 0],
            group_sem.at[sweep, 1],
            device_id=(i, in_line(0), k),
            device_id_type=MESH,
        )
        everyone.wait_recv()
        for s in range(group):
            gathered[sweep, j, pl.ds(s * twice, twice), :] = rx[sweep, s, 2 * limit :, :]

        def send_line(step):
            pltpu.make_async_remote_copy(
                gathered.at[sweep, j],
                gathered.at[sweep, j],
                line_sem.at[sweep, 0],
                line_sem.at[sweep, 1],
                device_id=(i, in_line(step), k),
                device_id_type=MESH,
            ).start()

        each(ny - 1, send_line)
        arrived = rx[sweep, 0, 0 : 2 * limit, :].astype(F32)
        for s in range(1, group):
            arrived = arrived + rx[sweep, s, 0 : 2 * limit, :].astype(F32)
        joint[0:limit, :] = jnp.concatenate(
            [arrived[:limit], arrived[limit:]], axis=1
        ).astype(BF16)

        if sweep == 0:
            lines = coarse.at[pl.ds(0, ny - 1)]
            pltpu.make_async_remote_copy(
                lines, lines, coarse_sem.at[0], coarse_sem.at[1],
                device_id=(i, in_line(0), k), device_id_type=MESH,
            ).wait()
            hots = hot.at[pl.ds(0, ny - 1)]
            pltpu.make_async_remote_copy(
                hots, hots, hot_sem.at[2], hot_sem.at[3],
                device_id=(i, in_line(0), k), device_id_type=MESH,
            ).wait()
            picks = jnp.where(ids == lane, 1.0, 0.0).astype(BF16)
            depth = width // ny
            chosen = jnp.zeros((twice, width), F32)
            for y in range(ny):
                chosen = chosen + jnp.dot(
                    picks[:, y * depth : (y + 1) * depth], coarse[y], preferred_element_type=F32
                )
            chosen = chosen.astype(BF16)
            span = group * twice
            upper = lax.broadcasted_iota(jnp.int32, (twice, span), 0) // count
            lower = lax.rem(lax.broadcasted_iota(jnp.int32, (twice, span), 1), twice) // count
            for y in range(ny):
                entries_y = lax.dot_general(
                    chosen, hot[y], (((1,), (1,)), ((), ())), preferred_element_type=F32
                )
                mixing[y] = jnp.where(upper == lower, entries_y, 0.0).astype(BF16)

        pltpu.make_async_remote_copy(
            gathered.at[sweep, pl.ds(0, ny - 1)],
            gathered.at[sweep, pl.ds(0, ny - 1)],
            line_sem.at[sweep, 0],
            line_sem.at[sweep, 1],
            device_id=(i, in_line(0), k),
            device_id_type=MESH,
        ).wait_recv()
        picked = jnp.zeros((twice, half), F32)
        for y in range(ny):
            picked = picked + jnp.dot(mixing[y], gathered[sweep, y], preferred_element_type=F32)
        picked = jnp.concatenate([picked[:count], picked[count:]], axis=1)
        joint[limit:, :] = jnp.concatenate(
            [picked, jnp.zeros((twice - count, columns), F32)], axis=0
        ).astype(BF16)

        for f in (4, 5, 2, 3, 0, 1):
            part = pl.ds(f * face, face)
            if f < 4:

                @pl.when(has(f))
                def _():
                    await_face(sweep, f)

            value = base[part, :] - jnp.dot(
                lifted[part, :], joint[...], preferred_element_type=F32
            )
            if f < 4:
                value = value + link[f].astype(F32) * face_in[sweep, f].astype(F32)
            final[part, :] = value
            rounded[part, :] = value.astype(BF16)
            if sweep == ITERS - 1:
                pltpu.make_async_copy(
                    final.at[part], out_hbm.at[part], store_sem.at[f]
                ).start()

    for f in range(6):
        part = pl.ds(f * face, face)
        field[part, :] = jnp.dot(
            inverse[part, :], rounded[...], preferred_element_type=F32
        ).astype(BF16)
        pltpu.make_async_copy(field.at[part], field_hbm.at[part], store_sem.at[6 + f]).start()

    for sweep in range(ITERS):
        for f in range(4):

            @pl.when(has(f))
            def _():
                face_copy(sweep, f).wait_send()

        pltpu.make_async_remote_copy(
            tx.at[sweep, pl.ds(0, group - 1)],
            rx.at[sweep, pl.ds(0, group - 1)],
            group_sem.at[sweep, 0],
            group_sem.at[sweep, 1],
            device_id=(i, in_line(0), k),
            device_id_type=MESH,
        ).wait_send()
        pltpu.make_async_remote_copy(
            gathered.at[sweep, pl.ds(0, ny - 1)],
            gathered.at[sweep, pl.ds(0, ny - 1)],
            line_sem.at[sweep, 0],
            line_sem.at[sweep, 1],
            device_id=(i, in_line(0), k),
            device_id_type=MESH,
        ).wait_send()
    for f in range(6):
        part = pl.ds(f * face, face)
        pltpu.make_async_copy(final.at[part], out_hbm.at[part], store_sem.at[f]).wait()
        pltpu.make_async_copy(field.at[part], field_hbm.at[part], store_sem.at[6 + f]).wait()


def body(
    right_side,
    interface_inverse,
    face_link,
    far_target,
    far_rank,
    far_basis,
    patch_basis,
    corner_basis,
    corner_row,
    coarse_inverse,
):
    nx, ny, nz = (lax.axis_size(name) for name in ("sx", "sy", "sz"))
    group = nx * nz
    order = interface_inverse.shape[-1]
    columns = right_side.shape[-1]
    face = order // 6
    entries, limit = far_basis.shape[-3:-1]
    count = corner_row.shape[-1]
    depth, width = coarse_inverse.shape
    twice = 2 * count
    half = columns // 2
    stack = group * limit + twice
    message = 2 * limit + twice
    smem = pl.BlockSpec(memory_space=pltpu.SMEM)
    anywhere = pl.BlockSpec(memory_space=pl.ANY)
    multipliers, field = pl.pallas_call(
        functools.partial(kernel, (nx, ny, nz)),
        out_shape=(
            jax.ShapeDtypeStruct((order, columns), F32),
            jax.ShapeDtypeStruct((order, columns), BF16),
        ),
        in_specs=[smem] * 4 + [anywhere] * 6,
        out_specs=(anywhere, anywhere),
        scratch_shapes=[
            pltpu.VMEM((order, columns), BF16),
            pltpu.VMEM((order, order), BF16),
            pltpu.VMEM((entries * limit, order), BF16),
            pltpu.VMEM((limit, order), BF16),
            pltpu.VMEM((count, order), BF16),
            pltpu.VMEM((ny, depth, width), BF16),
            pltpu.VMEM((stack, order), BF16),
            pltpu.VMEM((order, limit + twice), BF16),
            pltpu.VMEM((ny, group * twice, width), BF16),
            pltpu.VMEM((ny, twice, group * twice), BF16),
            pltpu.VMEM((order, columns), BF16),
            pltpu.VMEM((ITERS, order, columns), BF16),
            pltpu.VMEM((order, columns), F32),
            pltpu.VMEM((ITERS, 4, face, columns), BF16),
            pltpu.VMEM((ITERS, group, message, half), BF16),
            pltpu.VMEM((ITERS, group, message, half), BF16),
            pltpu.VMEM((ITERS, ny, group * twice, half), BF16),
            pltpu.VMEM((limit + twice, columns), BF16),
            pltpu.VMEM((order, columns), F32),
            pltpu.VMEM((order, columns), BF16),
            pltpu.SemaphoreType.DMA((11,)),
            pltpu.SemaphoreType.DMA((12,)),
            pltpu.SemaphoreType.DMA((4,)),
            pltpu.SemaphoreType.DMA((2,)),
            pltpu.SemaphoreType.DMA((ITERS, 4, 2)),
            pltpu.SemaphoreType.DMA((ITERS, 2)),
            pltpu.SemaphoreType.DMA((ITERS, 2)),
        ],
        compiler_params=pltpu.CompilerParams(
            collective_id=0, has_side_effects=True, vmem_limit_bytes=60 * 1024 * 1024
        ),
    )(
        face_link.reshape(-1),
        far_target.reshape(-1),
        far_rank.reshape(-1),
        corner_row.reshape(-1),
        right_side.reshape(order, columns),
        interface_inverse.reshape(order, order),
        far_basis.reshape(entries * limit, order),
        patch_basis.reshape(limit, order),
        corner_basis.reshape(count, order),
        coarse_inverse,
    )
    return multipliers.reshape(right_side.shape), field.reshape(right_side.shape)


def solution(mesh):
    wide = P("sx", "sy", "sz", None, None)
    return jax.shard_map(
        body,
        mesh=mesh,
        in_specs=(
            wide,
            wide,
            P("sx", "sy", "sz", None),
            wide,
            P("sx", "sy", "sz", None),
            P("sx", "sy", "sz", None, None, None),
            wide,
            wide,
            P("sx", "sy", "sz", None),
            P("sy", None),
        ),
        out_specs=(wide, wide),
        check_vma=False,
    )
```

```python
import functools

import jax
import jax.numpy as jnp
from jax import lax
from jax.experimental import pallas as pl
from jax.experimental.pallas import tpu as pltpu
from jax.sharding import PartitionSpec as P

ITERS = 2
F32 = jnp.float32
BF16 = jnp.bfloat16
MESH = pl.DeviceIdType.MESH


def each(count, step):
    if count <= 16:
        for number in range(count):
            step(number)
    else:

        @pl.loop(0, count)
        def _(number):
            step(number)


def kernel(
    sizes,
    link,
    target,
    rank,
    corner,
    right_hbm,
    inverse_hbm,
    bases_hbm,
    patch_hbm,
    corners_hbm,
    coarse_hbm,
    out_hbm,
    right,
    inverse,
    bases,
    patch,
    corners,
    coarse,
    stacked,
    early,
    lifted,
    names,
    every_name,
    hot,
    mixing,
    rounded,
    solved,
    base,
    face_in,
    tx,
    rx,
    gathered,
    joint,
    final,
    load_sem,
    store_sem,
    name_sem,
    coarse_sem,
    face_sem,
    group_sem,
    line_sem,
):
    nx, ny, nz = sizes
    group = nx * nz
    order, columns = right.shape
    face = order // 6
    entries = target.shape[0]
    limit = bases.shape[0] // entries
    count = corner.shape[0]
    twice = 2 * count
    half = columns // 2
    width = coarse.shape[-1]
    i, j, k = (lax.axis_index(name) for name in ("sx", "sy", "sz"))
    me = i * nz + k

    def member(step):
        other = lax.rem(me + 1 + step, group)
        return other // nz, lax.rem(other, nz)

    def in_line(step):
        return lax.rem(j + 1 + step, ny)

    loads = []

    def load(source, place):
        copy = pltpu.make_async_copy(source, place, load_sem.at[len(loads)])
        copy.start()
        loads.append(copy)
        return copy

    load_coarse = load(coarse_hbm, coarse.at[j])
    load_bases = load(bases_hbm, bases)
    load_patch = load(patch_hbm, patch)
    load_corners = load(corners_hbm, corners)
    load_right = load(right_hbm, right)
    load_rows = [
        load(inverse_hbm.at[pl.ds(f * face, face)], inverse.at[pl.ds(f * face, face)])
        for f in range(6)
    ]

    barrier = pltpu.get_barrier_semaphore()

    def greet(step):
        a, c = member(step)
        pl.semaphore_signal(barrier, inc=1, device_id=(a, j, c), device_id_type=MESH)

    def greet_line(step):
        pl.semaphore_signal(barrier, inc=1, device_id=(i, in_line(step), k), device_id_type=MESH)

    each(group - 1, greet)
    each(ny - 1, greet_line)

    row = lax.broadcasted_iota(jnp.int32, names.shape[1:], 0)
    spot = lax.broadcasted_iota(jnp.int32, names.shape[1:], 1)
    ids = jnp.zeros(names.shape[1:], jnp.int32)
    for q in range(count):
        ids = jnp.where(row == q, corner[q], ids)
    names[me] = jnp.where(spot == me, ids, 0).astype(F32)

    for number, axis_index, edge in ((0, i, 0), (1, i, nx - 1), (2, j, 0), (3, j, ny - 1)):

        @pl.when(axis_index == edge)
        def _():
            for sweep in range(ITERS):
                face_in[sweep, number] = jnp.zeros((face, columns), BF16)

    load_bases.wait()
    load_patch.wait()
    load_corners.wait()
    total = entries * limit
    block = min(group * limit, 128)
    lanes = lax.broadcasted_iota(jnp.int32, (1, total), 1)
    entry = lanes // limit
    named = jnp.zeros((1, total), jnp.int32)
    kept = jnp.zeros((1, total), jnp.int32)
    for e in range(entries):
        named = jnp.where(entry == e, target[e], named)
        kept = jnp.where(entry == e, rank[e], kept)
    place = lax.rem(lanes, limit)
    wanted = jnp.where(place < kept, named * limit + place, -1)
    for start in range(0, group * limit, block):
        rows = lax.broadcasted_iota(jnp.int32, (block, total), 0) + start
        route = jnp.where(rows == wanted, 1.0, 0.0).astype(BF16)
        stacked[pl.ds(start, block), :] = jnp.dot(
            route, bases[...], preferred_element_type=F32
        ).astype(BF16)
    padded = jnp.concatenate(
        [corners[...].astype(F32), jnp.zeros((twice - count, order), F32)], axis=0
    )
    stacked[pl.ds(group * limit, twice), :] = padded.astype(BF16)
    lifted[...] = jnp.transpose(
        jnp.concatenate([patch[...].astype(F32), padded], axis=0)
    ).astype(BF16)

    pl.semaphore_wait(barrier, group - 1 + ny - 1)

    def send_names(step):
        a, c = member(step)
        pltpu.make_async_remote_copy(
            names.at[me], names.at[me], name_sem.at[0], name_sem.at[1],
            device_id=(a, j, c), device_id_type=MESH,
        ).start()

    each(group - 1, send_names)
    load_coarse.wait()

    def send_coarse(step):
        pltpu.make_async_remote_copy(
            coarse.at[j],
            coarse.at[j],
            coarse_sem.at[0],
            coarse_sem.at[1],
            device_id=(i, in_line(step), k),
            device_id_type=MESH,
        ).start()

    each(ny - 1, send_coarse)

    load_right.wait()
    rounded[...] = right[...]

    def face_copy(sweep, f):
        if f < 2:
            to = (i + (1 if f == 1 else -1), j, k)
        else:
            to = (i, j + (1 if f == 3 else -1), k)
        return pltpu.make_async_remote_copy(
            solved.at[sweep, pl.ds(f * face, face)],
            face_in.at[sweep, f ^ 1],
            face_sem.at[sweep, f, 0],
            face_sem.at[sweep, f ^ 1, 1],
            device_id=to,
            device_id_type=MESH,
        )

    def await_face(sweep, f):
        to = ((i - 1, j, k), (i + 1, j, k), (i, j - 1, k), (i, j + 1, k))[f]
        pltpu.make_async_remote_copy(
            solved.at[sweep, pl.ds((f ^ 1) * face, face)],
            face_in.at[sweep, f],
            face_sem.at[sweep, f ^ 1, 0],
            face_sem.at[sweep, f, 1],
            device_id=to,
            device_id_type=MESH,
        ).wait_recv()

    def has(f):
        return (i > 0, i < nx - 1, j > 0, j < ny - 1)[f]

    def send_face(sweep, f):
        @pl.when(has(f))
        def _():
            face_copy(sweep, f).start()

    def pack(sweep, coefficient):
        terms = coefficient[group * limit : group * limit + count]
        terms = jnp.concatenate([terms[:, :half], terms[:, half:]], axis=0).astype(BF16)
        for t in range(group):
            own = coefficient[t * limit : (t + 1) * limit].astype(BF16)
            tx[sweep, t, 0:limit, :] = own[:, :half]
            tx[sweep, t, limit : 2 * limit, :] = own[:, half:]
            tx[sweep, t, 2 * limit :, :] = terms

        def send_group(step):
            a, c = member(step)
            pltpu.make_async_remote_copy(
                tx.at[sweep, a * nz + c],
                rx.at[sweep, me],
                group_sem.at[sweep, 0],
                group_sem.at[sweep, 1],
                device_id=(a, j, c),
                device_id_type=MESH,
            ).start()

        each(group - 1, send_group)
        rx[sweep, me] = tx[sweep, me]

    for sweep in range(ITERS):
        if sweep > 0:
            pack(sweep, jnp.dot(early[...], rounded[...], preferred_element_type=F32))
        for f in range(6):
            if sweep == 0:
                load_rows[f].wait()
            part = pl.ds(f * face, face)
            product = jnp.dot(
                inverse[part, :], rounded[...], preferred_element_type=F32
            ).astype(BF16)
            solved[sweep, part, :] = product
            if f < 4:
                send_face(sweep, f)

        if sweep == 0:
            pack(sweep, jnp.dot(stacked[...], solved[sweep], preferred_element_type=F32))
            others = names.at[pl.ds(0, group - 1)]
            pltpu.make_async_remote_copy(
                others, others, name_sem.at[0], name_sem.at[1],
                device_id=(i, in_line(0), k), device_id_type=MESH,
            ).wait()
            every_name[j] = jnp.sum(names[...], axis=0)

            def send_line_names(step):
                pltpu.make_async_remote_copy(
                    every_name.at[j], every_name.at[j], name_sem.at[2], name_sem.at[3],
                    device_id=(i, in_line(step), k), device_id_type=MESH,
                ).start()

            each(ny - 1, send_line_names)

        for f in range(6):
            part = pl.ds(f * face, face)
            value = solved[sweep, part, :].astype(F32)
            source = right[part, :].astype(F32)
            before = source if sweep == 0 else final[part, :]
            base[part, :] = before + source - value

        everyone = pltpu.make_async_remote_copy(
            tx.at[sweep, pl.ds(0, group - 1)],
            rx.at[sweep, pl.ds(0, group - 1)],
            group_sem.at[sweep, 0],
            group_sem.at[sweep, 1],
            device_id=(i, in_line(0), k),
            device_id_type=MESH,
        )
        everyone.wait_recv()
        for s in range(group):
            gathered[sweep, j, pl.ds(s * twice, twice), :] = rx[sweep, s, 2 * limit :, :]

        def send_line(step):
            pltpu.make_async_remote_copy(
                gathered.at[sweep, j],
                gathered.at[sweep, j],
                line_sem.at[sweep, 0],
                line_sem.at[sweep, 1],
                device_id=(i, in_line(step), k),
                device_id_type=MESH,
            ).start()

        each(ny - 1, send_line)
        arrived = rx[sweep, 0, 0 : 2 * limit, :].astype(F32)
        for s in range(1, group):
            arrived = arrived + rx[sweep, s, 0 : 2 * limit, :].astype(F32)
        joint[0:limit, :] = jnp.concatenate(
            [arrived[:limit], arrived[limit:]], axis=1
        ).astype(BF16)

        if sweep == 0:
            lines = coarse.at[pl.ds(0, ny - 1)]
            pltpu.make_async_remote_copy(
                lines, lines, coarse_sem.at[0], coarse_sem.at[1],
                device_id=(i, in_line(0), k), device_id_type=MESH,
            ).wait()
            lines = every_name.at[pl.ds(0, ny - 1)]
            pltpu.make_async_remote_copy(
                lines, lines, name_sem.at[2], name_sem.at[3],
                device_id=(i, in_line(0), k), device_id_type=MESH,
            ).wait()
            for n in range(6):
                part = pl.ds(n * face, face)
                early[:, part] = jnp.dot(
                    stacked[...], inverse[:, part], preferred_element_type=F32
                ).astype(BF16)
            row = lax.broadcasted_iota(jnp.int32, (twice, width), 0)
            lane = lax.broadcasted_iota(jnp.int32, (twice, width), 1)
            ids = jnp.zeros((twice, width), jnp.int32)
            for q in range(count):
                ids = jnp.where(lax.rem(row, count) == q, corner[q], ids)
            numbers = lax.broadcasted_iota(jnp.int32, (count, width), 1).astype(F32)
            picks = jnp.where(ids == lane, 1.0, 0.0).astype(BF16)
            depth = width // ny
            chosen = jnp.zeros((twice, width), F32)
            for y in range(ny):
                chosen = chosen + jnp.dot(
                    picks[:, y * depth : (y + 1) * depth], coarse[y], preferred_element_type=F32
                )
            chosen = chosen.astype(BF16)
            span = group * twice
            upper = lax.broadcasted_iota(jnp.int32, (twice, span), 0) // count
            lower = lax.rem(lax.broadcasted_iota(jnp.int32, (twice, span), 1), twice) // count
            for y in range(ny):
                named_y = every_name[y]
                for s in range(group):
                    one = jnp.where(named_y[:, s : s + 1] == numbers, 1.0, 0.0)
                    hot[pl.ds(s * twice, twice), :] = jnp.concatenate(
                        [one, one], axis=0
                    ).astype(BF16)
                entries_y = lax.dot_general(
                    chosen, hot[...], (((1,), (1,)), ((), ())), preferred_element_type=F32
                )
                mixing[y] = jnp.where(upper == lower, entries_y, 0.0).astype(BF16)

        pltpu.make_async_remote_copy(
            gathered.at[sweep, pl.ds(0, ny - 1)],
            gathered.at[sweep, pl.ds(0, ny - 1)],
            line_sem.at[sweep, 0],
            line_sem.at[sweep, 1],
            device_id=(i, in_line(0), k),
            device_id_type=MESH,
        ).wait_recv()
        picked = jnp.zeros((twice, half), F32)
        for y in range(ny):
            picked = picked + jnp.dot(mixing[y], gathered[sweep, y], preferred_element_type=F32)
        picked = jnp.concatenate([picked[:count], picked[count:]], axis=1)
        joint[limit:, :] = jnp.concatenate(
            [picked, jnp.zeros((twice - count, columns), F32)], axis=0
        ).astype(BF16)

        for f in (4, 5, 2, 3, 0, 1):
            part = pl.ds(f * face, face)
            if f < 4:

                @pl.when(has(f))
                def _():
                    await_face(sweep, f)

            value = base[part, :] - jnp.dot(
                lifted[part, :], joint[...], preferred_element_type=F32
            )
            if f < 4:
                value = value + link[f].astype(F32) * face_in[sweep, f].astype(F32)
            final[part, :] = value
            rounded[part, :] = value.astype(BF16)
            if sweep == ITERS - 1:
                pltpu.make_async_copy(
                    final.at[part], out_hbm.at[part], store_sem.at[f]
                ).start()

    for sweep in range(ITERS):
        for f in range(4):

            @pl.when(has(f))
            def _():
                face_copy(sweep, f).wait_send()

        pltpu.make_async_remote_copy(
            tx.at[sweep, pl.ds(0, group - 1)],
            rx.at[sweep, pl.ds(0, group - 1)],
            group_sem.at[sweep, 0],
            group_sem.at[sweep, 1],
            device_id=(i, in_line(0), k),
            device_id_type=MESH,
        ).wait_send()
        pltpu.make_async_remote_copy(
            gathered.at[sweep, pl.ds(0, ny - 1)],
            gathered.at[sweep, pl.ds(0, ny - 1)],
            line_sem.at[sweep, 0],
            line_sem.at[sweep, 1],
            device_id=(i, in_line(0), k),
            device_id_type=MESH,
        ).wait_send()
    for f in range(6):
        part = pl.ds(f * face, face)
        pltpu.make_async_copy(final.at[part], out_hbm.at[part], store_sem.at[f]).wait()


def last_kernel(inverse_hbm, values_hbm, out_hbm, field_hbm, inverse, values, rounded, field, load_sem, store_sem):
    face = inverse.shape[0] // 6
    first = pltpu.make_async_copy(values_hbm, values, load_sem.at[6])
    first.start()
    parts = [pl.ds(f * face, face) for f in range(6)]
    loads = [
        pltpu.make_async_copy(inverse_hbm.at[part], inverse.at[part], load_sem.at[f])
        for f, part in enumerate(parts)
    ]
    for copy in loads:
        copy.start()
    first.wait()
    stores = [pltpu.make_async_copy(values, out_hbm, store_sem.at[6])]
    stores[0].start()
    rounded[...] = values[...].astype(BF16)
    for f, part in enumerate(parts):
        loads[f].wait()
        field[part, :] = jnp.dot(
            inverse[part, :], rounded[...], preferred_element_type=F32
        ).astype(BF16)
        copy = pltpu.make_async_copy(field.at[part], field_hbm.at[part], store_sem.at[f])
        copy.start()
        stores.append(copy)
    for copy in stores:
        copy.wait()


def body(
    right_side,
    interface_inverse,
    face_link,
    far_target,
    far_rank,
    far_basis,
    patch_basis,
    corner_basis,
    corner_row,
    coarse_inverse,
):
    nx, ny, nz = (lax.axis_size(name) for name in ("sx", "sy", "sz"))
    group = nx * nz
    order = interface_inverse.shape[-1]
    columns = right_side.shape[-1]
    face = order // 6
    entries, limit = far_basis.shape[-3:-1]
    count = corner_row.shape[-1]
    depth, width = coarse_inverse.shape
    twice = 2 * count
    half = columns // 2
    stack = group * limit + twice
    message = 2 * limit + twice
    lanes = -(-group // 128) * 128
    smem = pl.BlockSpec(memory_space=pltpu.SMEM)
    anywhere = pl.BlockSpec(memory_space=pl.ANY)
    matrix = interface_inverse.reshape(order, order)
    multipliers = pl.pallas_call(
        functools.partial(kernel, (nx, ny, nz)),
        out_shape=jax.ShapeDtypeStruct((order, columns), F32),
        in_specs=[smem] * 4 + [anywhere] * 6,
        out_specs=anywhere,
        scratch_shapes=[
            pltpu.VMEM((order, columns), BF16),
            pltpu.VMEM((order, order), BF16),
            pltpu.VMEM((entries * limit, order), BF16),
            pltpu.VMEM((limit, order), BF16),
            pltpu.VMEM((count, order), BF16),
            pltpu.VMEM((ny, depth, width), BF16),
            pltpu.VMEM((stack, order), BF16),
            pltpu.VMEM((stack, order), BF16),
            pltpu.VMEM((order, limit + twice), BF16),
            pltpu.VMEM((group, count, lanes), F32),
            pltpu.VMEM((ny, count, lanes), F32),
            pltpu.VMEM((group * twice, width), BF16),
            pltpu.VMEM((ny, twice, group * twice), BF16),
            pltpu.VMEM((order, columns), BF16),
            pltpu.VMEM((ITERS, order, columns), BF16),
            pltpu.VMEM((order, columns), F32),
            pltpu.VMEM((ITERS, 4, face, columns), BF16),
            pltpu.VMEM((ITERS, group, message, half), BF16),
            pltpu.VMEM((ITERS, group, message, half), BF16),
            pltpu.VMEM((ITERS, ny, group * twice, half), BF16),
            pltpu.VMEM((limit + twice, columns), BF16),
            pltpu.VMEM((order, columns), F32),
            pltpu.SemaphoreType.DMA((11,)),
            pltpu.SemaphoreType.DMA((6,)),
            pltpu.SemaphoreType.DMA((4,)),
            pltpu.SemaphoreType.DMA((2,)),
            pltpu.SemaphoreType.DMA((ITERS, 4, 2)),
            pltpu.SemaphoreType.DMA((ITERS, 2)),
            pltpu.SemaphoreType.DMA((ITERS, 2)),
        ],
        compiler_params=pltpu.CompilerParams(
            collective_id=0, has_side_effects=True, vmem_limit_bytes=60 * 1024 * 1024
        ),
    )(
        face_link.reshape(-1),
        far_target.reshape(-1),
        far_rank.reshape(-1),
        corner_row.reshape(-1),
        right_side.reshape(order, columns),
        matrix,
        far_basis.reshape(entries * limit, order),
        patch_basis.reshape(limit, order),
        corner_basis.reshape(count, order),
        coarse_inverse,
    )
    multipliers, field = pl.pallas_call(
        last_kernel,
        out_shape=(
            jax.ShapeDtypeStruct((order, columns), F32),
            jax.ShapeDtypeStruct((order, columns), BF16),
        ),
        in_specs=[anywhere] * 2,
        out_specs=(anywhere, anywhere),
        scratch_shapes=[
            pltpu.VMEM((order, order), BF16),
            pltpu.VMEM((order, columns), F32),
            pltpu.VMEM((order, columns), BF16),
            pltpu.VMEM((order, columns), BF16),
            pltpu.SemaphoreType.DMA((7,)),
            pltpu.SemaphoreType.DMA((7,)),
        ],
        compiler_params=pltpu.CompilerParams(vmem_limit_bytes=24 * 1024 * 1024),
    )(matrix, multipliers)
    return multipliers.reshape(right_side.shape), field.reshape(right_side.shape)


def solution(mesh):
    wide = P("sx", "sy", "sz", None, None)
    return jax.shard_map(
        body,
        mesh=mesh,
        in_specs=(
            wide,
            wide,
            P("sx", "sy", "sz", None),
            wide,
            P("sx", "sy", "sz", None),
            P("sx", "sy", "sz", None, None, None),
            wide,
            wide,
            P("sx", "sy", "sz", None),
            P("sy", None),
        ),
        out_specs=(wide, wide),
        check_vma=False,
    )
```

```python
import functools

import jax
import jax.numpy as jnp
from jax import lax
from jax.experimental import pallas as pl
from jax.experimental.pallas import tpu as pltpu
from jax.sharding import PartitionSpec as P

ITERS = 2
F32 = jnp.float32
BF16 = jnp.bfloat16
MESH = pl.DeviceIdType.MESH


def each(count, step):
    if count <= 16:
        for number in range(count):
            step(number)
    else:

        @pl.loop(0, count)
        def _(number):
            step(number)


def kernel(
    sizes,
    link,
    target,
    rank,
    corner,
    right_hbm,
    inverse_hbm,
    bases_hbm,
    patch_hbm,
    corners_hbm,
    coarse_hbm,
    final,
    field,
    right,
    inverse,
    bases,
    patch,
    corners,
    coarse,
    stacked,
    early,
    lifted,
    names,
    every_name,
    hot,
    mixing,
    rounded,
    solved,
    base,
    face_in,
    tx,
    rx,
    gathered,
    joint,
    load_sem,
    name_sem,
    coarse_sem,
    face_sem,
    group_sem,
    line_sem,
):
    nx, ny, nz = sizes
    group = nx * nz
    order, columns = right.shape
    face = order // 6
    entries = target.shape[0]
    limit = bases.shape[0] // entries
    count = corner.shape[0]
    twice = 2 * count
    half = columns // 2
    width = coarse.shape[-1]
    i, j, k = (lax.axis_index(name) for name in ("sx", "sy", "sz"))
    me = i * nz + k

    def member(step):
        other = lax.rem(me + 1 + step, group)
        return other // nz, lax.rem(other, nz)

    def in_line(step):
        return lax.rem(j + 1 + step, ny)

    loads = []

    def load(source, place):
        copy = pltpu.make_async_copy(source, place, load_sem.at[len(loads)])
        copy.start()
        loads.append(copy)
        return copy

    load_coarse = load(coarse_hbm, coarse.at[j])
    load_bases = load(bases_hbm, bases)
    load_patch = load(patch_hbm, patch)
    load_corners = load(corners_hbm, corners)
    load_right = load(right_hbm, right)
    load_rows = [
        load(inverse_hbm.at[pl.ds(f * face, face)], inverse.at[pl.ds(f * face, face)])
        for f in range(6)
    ]

    barrier = pltpu.get_barrier_semaphore()

    def greet(step):
        a, c = member(step)
        pl.semaphore_signal(barrier, inc=1, device_id=(a, j, c), device_id_type=MESH)

    def greet_line(step):
        pl.semaphore_signal(barrier, inc=1, device_id=(i, in_line(step), k), device_id_type=MESH)

    each(group - 1, greet)
    each(ny - 1, greet_line)

    row = lax.broadcasted_iota(jnp.int32, names.shape[1:], 0)
    spot = lax.broadcasted_iota(jnp.int32, names.shape[1:], 1)
    ids = jnp.zeros(names.shape[1:], jnp.int32)
    for q in range(count):
        ids = jnp.where(row == q, corner[q], ids)
    names[me] = jnp.where(spot == me, ids, 0).astype(F32)

    for number, axis_index, edge in ((0, i, 0), (1, i, nx - 1), (2, j, 0), (3, j, ny - 1)):

        @pl.when(axis_index == edge)
        def _():
            for sweep in range(ITERS):
                face_in[sweep, number] = jnp.zeros((face, columns), BF16)

    load_bases.wait()
    load_patch.wait()
    load_corners.wait()
    total = entries * limit
    block = min(group * limit, 128)
    lanes = lax.broadcasted_iota(jnp.int32, (1, total), 1)
    entry = lanes // limit
    named = jnp.zeros((1, total), jnp.int32)
    kept = jnp.zeros((1, total), jnp.int32)
    for e in range(entries):
        named = jnp.where(entry == e, target[e], named)
        kept = jnp.where(entry == e, rank[e], kept)
    place = lax.rem(lanes, limit)
    wanted = jnp.where(place < kept, named * limit + place, -1)
    for start in range(0, group * limit, block):
        rows = lax.broadcasted_iota(jnp.int32, (block, total), 0) + start
        route = jnp.where(rows == wanted, 1.0, 0.0).astype(BF16)
        stacked[pl.ds(start, block), :] = jnp.dot(
            route, bases[...], preferred_element_type=F32
        ).astype(BF16)
    padded = jnp.concatenate(
        [corners[...].astype(F32), jnp.zeros((twice - count, order), F32)], axis=0
    )
    stacked[pl.ds(group * limit, twice), :] = padded.astype(BF16)
    lifted[...] = jnp.transpose(
        jnp.concatenate([patch[...].astype(F32), padded], axis=0)
    ).astype(BF16)

    pl.semaphore_wait(barrier, group - 1 + ny - 1)

    def send_names(step):
        a, c = member(step)
        pltpu.make_async_remote_copy(
            names.at[me], names.at[me], name_sem.at[0], name_sem.at[1],
            device_id=(a, j, c), device_id_type=MESH,
        ).start()

    each(group - 1, send_names)
    load_coarse.wait()

    def send_coarse(step):
        pltpu.make_async_remote_copy(
            coarse.at[j],
            coarse.at[j],
            coarse_sem.at[0],
            coarse_sem.at[1],
            device_id=(i, in_line(step), k),
            device_id_type=MESH,
        ).start()

    each(ny - 1, send_coarse)

    load_right.wait()
    rounded[...] = right[...]

    def face_copy(sweep, f):
        if f < 2:
            to = (i + (1 if f == 1 else -1), j, k)
        else:
            to = (i, j + (1 if f == 3 else -1), k)
        return pltpu.make_async_remote_copy(
            solved.at[sweep, pl.ds(f * face, face)],
            face_in.at[sweep, f ^ 1],
            face_sem.at[sweep, f, 0],
            face_sem.at[sweep, f ^ 1, 1],
            device_id=to,
            device_id_type=MESH,
        )

    def await_face(sweep, f):
        to = ((i - 1, j, k), (i + 1, j, k), (i, j - 1, k), (i, j + 1, k))[f]
        pltpu.make_async_remote_copy(
            solved.at[sweep, pl.ds((f ^ 1) * face, face)],
            face_in.at[sweep, f],
            face_sem.at[sweep, f ^ 1, 0],
            face_sem.at[sweep, f, 1],
            device_id=to,
            device_id_type=MESH,
        ).wait_recv()

    def has(f):
        return (i > 0, i < nx - 1, j > 0, j < ny - 1)[f]

    def send_face(sweep, f):
        @pl.when(has(f))
        def _():
            face_copy(sweep, f).start()

    def pack(sweep, coefficient):
        terms = coefficient[group * limit : group * limit + count]
        terms = jnp.concatenate([terms[:, :half], terms[:, half:]], axis=0).astype(BF16)
        for t in range(group):
            own = coefficient[t * limit : (t + 1) * limit].astype(BF16)
            tx[sweep, t, 0:limit, :] = own[:, :half]
            tx[sweep, t, limit : 2 * limit, :] = own[:, half:]
            tx[sweep, t, 2 * limit :, :] = terms

        def send_group(step):
            a, c = member(step)
            pltpu.make_async_remote_copy(
                tx.at[sweep, a * nz + c],
                rx.at[sweep, me],
                group_sem.at[sweep, 0],
                group_sem.at[sweep, 1],
                device_id=(a, j, c),
                device_id_type=MESH,
            ).start()

        each(group - 1, send_group)
        rx[sweep, me] = tx[sweep, me]

    def forward(sweep):
        everyone = pltpu.make_async_remote_copy(
            tx.at[sweep, pl.ds(0, group - 1)],
            rx.at[sweep, pl.ds(0, group - 1)],
            group_sem.at[sweep, 0],
            group_sem.at[sweep, 1],
            device_id=(i, in_line(0), k),
            device_id_type=MESH,
        )
        everyone.wait_recv()
        for s in range(group):
            gathered[sweep, j, pl.ds(s * twice, twice), :] = rx[sweep, s, 2 * limit :, :]

        def send_line(step):
            pltpu.make_async_remote_copy(
                gathered.at[sweep, j],
                gathered.at[sweep, j],
                line_sem.at[sweep, 0],
                line_sem.at[sweep, 1],
                device_id=(i, in_line(step), k),
                device_id_type=MESH,
            ).start()

        each(ny - 1, send_line)
        arrived = rx[sweep, 0, 0 : 2 * limit, :].astype(F32)
        for s in range(1, group):
            arrived = arrived + rx[sweep, s, 0 : 2 * limit, :].astype(F32)
        joint[0:limit, :] = jnp.concatenate(
            [arrived[:limit], arrived[limit:]], axis=1
        ).astype(BF16)

    for sweep in range(ITERS):
        if sweep > 0:
            pack(sweep, jnp.dot(early[...], rounded[...], preferred_element_type=F32))
        for f in range(6):
            if sweep == 0:
                load_rows[f].wait()
            part = pl.ds(f * face, face)
            product = jnp.dot(
                inverse[part, :], rounded[...], preferred_element_type=F32
            ).astype(BF16)
            solved[sweep, part, :] = product
            if f < 4:
                send_face(sweep, f)
            if f == 4 and sweep > 0:
                forward(sweep)

        if sweep == 0:
            pack(sweep, jnp.dot(stacked[...], solved[sweep], preferred_element_type=F32))
            others = names.at[pl.ds(0, group - 1)]
            pltpu.make_async_remote_copy(
                others, others, name_sem.at[0], name_sem.at[1],
                device_id=(i, in_line(0), k), device_id_type=MESH,
            ).wait()
            every_name[j] = jnp.sum(names[...], axis=0)

            def send_line_names(step):
                pltpu.make_async_remote_copy(
                    every_name.at[j], every_name.at[j], name_sem.at[2], name_sem.at[3],
                    device_id=(i, in_line(step), k), device_id_type=MESH,
                ).start()

            each(ny - 1, send_line_names)

        for f in range(6):
            part = pl.ds(f * face, face)
            value = solved[sweep, part, :].astype(F32)
            source = right[part, :].astype(F32)
            before = source if sweep == 0 else final[part, :]
            base[part, :] = before + source - value

        if sweep == 0:
            forward(sweep)

        if sweep == 0:
            lines = coarse.at[pl.ds(0, ny - 1)]
            pltpu.make_async_remote_copy(
                lines, lines, coarse_sem.at[0], coarse_sem.at[1],
                device_id=(i, in_line(0), k), device_id_type=MESH,
            ).wait()
            lines = every_name.at[pl.ds(0, ny - 1)]
            pltpu.make_async_remote_copy(
                lines, lines, name_sem.at[2], name_sem.at[3],
                device_id=(i, in_line(0), k), device_id_type=MESH,
            ).wait()
            for n in range(6):
                part = pl.ds(n * face, face)
                early[:, part] = jnp.dot(
                    stacked[...], inverse[:, part], preferred_element_type=F32
                ).astype(BF16)
            row = lax.broadcasted_iota(jnp.int32, (twice, width), 0)
            lane = lax.broadcasted_iota(jnp.int32, (twice, width), 1)
            ids = jnp.zeros((twice, width), jnp.int32)
            for q in range(count):
                ids = jnp.where(lax.rem(row, count) == q, corner[q], ids)
            numbers = lax.broadcasted_iota(jnp.int32, (count, width), 1).astype(F32)
            picks = jnp.where(ids == lane, 1.0, 0.0).astype(BF16)
            depth = width // ny
            chosen = jnp.zeros((twice, width), F32)
            for y in range(ny):
                chosen = chosen + jnp.dot(
                    picks[:, y * depth : (y + 1) * depth], coarse[y], preferred_element_type=F32
                )
            chosen = chosen.astype(BF16)
            span = group * twice
            upper = lax.broadcasted_iota(jnp.int32, (twice, span), 0) // count
            lower = lax.rem(lax.broadcasted_iota(jnp.int32, (twice, span), 1), twice) // count
            for y in range(ny):
                named_y = every_name[y]
                for s in range(group):
                    one = jnp.where(named_y[:, s : s + 1] == numbers, 1.0, 0.0)
                    hot[pl.ds(s * twice, twice), :] = jnp.concatenate(
                        [one, one], axis=0
                    ).astype(BF16)
                entries_y = lax.dot_general(
                    chosen, hot[...], (((1,), (1,)), ((), ())), preferred_element_type=F32
                )
                mixing[y] = jnp.where(upper == lower, entries_y, 0.0).astype(BF16)

        pltpu.make_async_remote_copy(
            gathered.at[sweep, pl.ds(0, ny - 1)],
            gathered.at[sweep, pl.ds(0, ny - 1)],
            line_sem.at[sweep, 0],
            line_sem.at[sweep, 1],
            device_id=(i, in_line(0), k),
            device_id_type=MESH,
        ).wait_recv()
        picked = jnp.zeros((twice, half), F32)
        for y in range(ny):
            picked = picked + jnp.dot(mixing[y], gathered[sweep, y], preferred_element_type=F32)
        picked = jnp.concatenate([picked[:count], picked[count:]], axis=1)
        joint[limit:, :] = jnp.concatenate(
            [picked, jnp.zeros((twice - count, columns), F32)], axis=0
        ).astype(BF16)

        for f in (4, 5, 2, 3, 0, 1):
            part = pl.ds(f * face, face)
            if f < 4:

                @pl.when(has(f))
                def _():
                    await_face(sweep, f)

            value = base[part, :] - jnp.dot(
                lifted[part, :], joint[...], preferred_element_type=F32
            )
            if f < 4:
                value = value + link[f].astype(F32) * face_in[sweep, f].astype(F32)
            final[part, :] = value
            rounded[part, :] = value.astype(BF16)

    for f in range(6):
        part = pl.ds(f * face, face)
        field[part, :] = jnp.dot(
            inverse[part, :], rounded[...], preferred_element_type=F32
        ).astype(BF16)

    for sweep in range(ITERS):
        for f in range(4):

            @pl.when(has(f))
            def _():
                face_copy(sweep, f).wait_send()

        pltpu.make_async_remote_copy(
            tx.at[sweep, pl.ds(0, group - 1)],
            rx.at[sweep, pl.ds(0, group - 1)],
            group_sem.at[sweep, 0],
            group_sem.at[sweep, 1],
            device_id=(i, in_line(0), k),
            device_id_type=MESH,
        ).wait_send()
        pltpu.make_async_remote_copy(
            gathered.at[sweep, pl.ds(0, ny - 1)],
            gathered.at[sweep, pl.ds(0, ny - 1)],
            line_sem.at[sweep, 0],
            line_sem.at[sweep, 1],
            device_id=(i, in_line(0), k),
            device_id_type=MESH,
        ).wait_send()


def store_kernel(values, field, out_hbm, field_hbm, store_sem):
    copies = [
        pltpu.make_async_copy(values, out_hbm, store_sem.at[0]),
        pltpu.make_async_copy(field, field_hbm, store_sem.at[1]),
    ]
    for copy in copies:
        copy.start()
    for copy in copies:
        copy.wait()


def body(
    right_side,
    interface_inverse,
    face_link,
    far_target,
    far_rank,
    far_basis,
    patch_basis,
    corner_basis,
    corner_row,
    coarse_inverse,
):
    nx, ny, nz = (lax.axis_size(name) for name in ("sx", "sy", "sz"))
    group = nx * nz
    order = interface_inverse.shape[-1]
    columns = right_side.shape[-1]
    face = order // 6
    entries, limit = far_basis.shape[-3:-1]
    count = corner_row.shape[-1]
    depth, width = coarse_inverse.shape
    twice = 2 * count
    half = columns // 2
    stack = group * limit + twice
    message = 2 * limit + twice
    lanes = -(-group // 128) * 128
    smem = pl.BlockSpec(memory_space=pltpu.SMEM)
    hbm = pl.BlockSpec(memory_space=pl.ANY)
    scratch = [
        pltpu.VMEM((order, columns), BF16),
        pltpu.VMEM((order, order), BF16),
        pltpu.VMEM((entries * limit, order), BF16),
        pltpu.VMEM((limit, order), BF16),
        pltpu.VMEM((count, order), BF16),
        pltpu.VMEM((ny, depth, width), BF16),
        pltpu.VMEM((stack, order), BF16),
        pltpu.VMEM((stack, order), BF16),
        pltpu.VMEM((order, limit + twice), BF16),
        pltpu.VMEM((group, count, lanes), F32),
        pltpu.VMEM((ny, count, lanes), F32),
        pltpu.VMEM((group * twice, width), BF16),
        pltpu.VMEM((ny, twice, group * twice), BF16),
        pltpu.VMEM((order, columns), BF16),
        pltpu.VMEM((ITERS, order, columns), BF16),
        pltpu.VMEM((order, columns), F32),
        pltpu.VMEM((ITERS, 4, face, columns), BF16),
        pltpu.VMEM((ITERS, group, message, half), BF16),
        pltpu.VMEM((ITERS, group, message, half), BF16),
        pltpu.VMEM((ITERS, ny, group * twice, half), BF16),
        pltpu.VMEM((limit + twice, columns), BF16),
        pltpu.SemaphoreType.DMA((11,)),
        pltpu.SemaphoreType.DMA((4,)),
        pltpu.SemaphoreType.DMA((2,)),
        pltpu.SemaphoreType.DMA((ITERS, 4, 2)),
        pltpu.SemaphoreType.DMA((ITERS, 2)),
        pltpu.SemaphoreType.DMA((ITERS, 2)),
    ]
    vmem = pl.BlockSpec(memory_space=pltpu.VMEM)
    results = (
        jax.ShapeDtypeStruct((order, columns), F32),
        jax.ShapeDtypeStruct((order, columns), BF16),
    )
    multipliers, field = pl.pallas_call(
        functools.partial(kernel, (nx, ny, nz)),
        out_shape=results,
        in_specs=[smem] * 4 + [hbm] * 6,
        out_specs=(vmem, vmem),
        scratch_shapes=scratch,
        compiler_params=pltpu.CompilerParams(
            collective_id=0, has_side_effects=True, vmem_limit_bytes=48 * 1024 * 1024
        ),
    )(
        face_link.reshape(-1),
        far_target.reshape(-1),
        far_rank.reshape(-1),
        corner_row.reshape(-1),
        right_side.reshape(order, columns),
        interface_inverse.reshape(order, order),
        far_basis.reshape(entries * limit, order),
        patch_basis.reshape(limit, order),
        corner_basis.reshape(count, order),
        coarse_inverse,
    )
    multipliers, field = pl.pallas_call(
        store_kernel,
        out_shape=results,
        in_specs=[vmem] * 2,
        out_specs=(hbm, hbm),
        scratch_shapes=[pltpu.SemaphoreType.DMA((2,))],
    )(multipliers, field)
    return multipliers.reshape(right_side.shape), field.reshape(right_side.shape)


def solution(mesh):
    wide = P("sx", "sy", "sz", None, None)
    return jax.shard_map(
        body,
        mesh=mesh,
        in_specs=(
            wide,
            wide,
            P("sx", "sy", "sz", None),
            wide,
            P("sx", "sy", "sz", None),
            P("sx", "sy", "sz", None, None, None),
            wide,
            wide,
            P("sx", "sy", "sz", None),
            P("sy", None),
        ),
        out_specs=(wide, wide),
        check_vma=False,
    )
```

```python
import functools

import jax
import jax.numpy as jnp
from jax import lax
from jax.experimental import pallas as pl
from jax.experimental.pallas import tpu as pltpu
from jax.sharding import PartitionSpec as P

ITERS = 2
F32 = jnp.float32
BF16 = jnp.bfloat16
MESH = pl.DeviceIdType.MESH


def each(count, step):
    if count <= 16:
        for number in range(count):
            step(number)
    else:

        @pl.loop(0, count)
        def _(number):
            step(number)


def kernel(
    sizes,
    link,
    target,
    rank,
    corner,
    right_hbm,
    inverse_hbm,
    bases_hbm,
    patch_hbm,
    corners_hbm,
    coarse_hbm,
    out_hbm,
    field_hbm,
    right,
    inverse,
    bases,
    patch,
    corners,
    coarse,
    stacked,
    early,
    lifted,
    names,
    every_name,
    hot,
    mixing,
    rounded,
    solved,
    base,
    face_in,
    tx,
    rx,
    gathered,
    joint,
    final,
    field,
    load_sem,
    store_sem,
    name_sem,
    coarse_sem,
    face_sem,
    group_sem,
    line_sem,
):
    nx, ny, nz = sizes
    group = nx * nz
    order, columns = right.shape
    face = order // 6
    entries = target.shape[0]
    limit = bases.shape[0] // entries
    count = corner.shape[0]
    twice = 2 * count
    half = columns // 2
    width = coarse.shape[-1]
    i, j, k = (lax.axis_index(name) for name in ("sx", "sy", "sz"))
    me = i * nz + k

    def member(step):
        other = lax.rem(me + 1 + step, group)
        return other // nz, lax.rem(other, nz)

    def in_line(step):
        return lax.rem(j + 1 + step, ny)

    loads = []

    def load(source, place):
        copy = pltpu.make_async_copy(source, place, load_sem.at[len(loads)])
        copy.start()
        loads.append(copy)
        return copy

    load_coarse = load(coarse_hbm, coarse.at[j])
    load_bases = load(bases_hbm, bases)
    load_patch = load(patch_hbm, patch)
    load_corners = load(corners_hbm, corners)
    load_right = load(right_hbm, right)
    load_rows = [
        load(inverse_hbm.at[pl.ds(f * face, face)], inverse.at[pl.ds(f * face, face)])
        for f in range(6)
    ]

    barrier = pltpu.get_barrier_semaphore()

    def greet(step):
        a, c = member(step)
        pl.semaphore_signal(barrier, inc=1, device_id=(a, j, c), device_id_type=MESH)

    def greet_line(step):
        pl.semaphore_signal(barrier, inc=1, device_id=(i, in_line(step), k), device_id_type=MESH)

    each(group - 1, greet)
    each(ny - 1, greet_line)

    row = lax.broadcasted_iota(jnp.int32, names.shape[1:], 0)
    spot = lax.broadcasted_iota(jnp.int32, names.shape[1:], 1)
    ids = jnp.zeros(names.shape[1:], jnp.int32)
    for q in range(count):
        ids = jnp.where(row == q, corner[q], ids)
    names[me] = jnp.where(spot == me, ids, 0).astype(F32)

    for number, axis_index, edge in ((0, i, 0), (1, i, nx - 1), (2, j, 0), (3, j, ny - 1)):

        @pl.when(axis_index == edge)
        def _():
            for sweep in range(ITERS):
                face_in[sweep, number] = jnp.zeros((face, columns), BF16)

    load_bases.wait()
    load_patch.wait()
    load_corners.wait()
    total = entries * limit
    block = min(group * limit, 128)
    lanes = lax.broadcasted_iota(jnp.int32, (1, total), 1)
    entry = lanes // limit
    named = jnp.zeros((1, total), jnp.int32)
    kept = jnp.zeros((1, total), jnp.int32)
    for e in range(entries):
        named = jnp.where(entry == e, target[e], named)
        kept = jnp.where(entry == e, rank[e], kept)
    place = lax.rem(lanes, limit)
    wanted = jnp.where(place < kept, named * limit + place, -1)
    for start in range(0, group * limit, block):
        rows = lax.broadcasted_iota(jnp.int32, (block, total), 0) + start
        route = jnp.where(rows == wanted, 1.0, 0.0).astype(BF16)
        stacked[pl.ds(start, block), :] = jnp.dot(
            route, bases[...], preferred_element_type=F32
        ).astype(BF16)
    padded = jnp.concatenate(
        [corners[...].astype(F32), jnp.zeros((twice - count, order), F32)], axis=0
    )
    stacked[pl.ds(group * limit, twice), :] = padded.astype(BF16)
    lifted[...] = jnp.transpose(
        jnp.concatenate([patch[...].astype(F32), padded], axis=0)
    ).astype(BF16)

    pl.semaphore_wait(barrier, group - 1 + ny - 1)

    def send_names(step):
        a, c = member(step)
        pltpu.make_async_remote_copy(
            names.at[me], names.at[me], name_sem.at[0], name_sem.at[1],
            device_id=(a, j, c), device_id_type=MESH,
        ).start()

    each(group - 1, send_names)
    load_coarse.wait()

    def send_coarse(step):
        pltpu.make_async_remote_copy(
            coarse.at[j],
            coarse.at[j],
            coarse_sem.at[0],
            coarse_sem.at[1],
            device_id=(i, in_line(step), k),
            device_id_type=MESH,
        ).start()

    each(ny - 1, send_coarse)

    load_right.wait()
    rounded[...] = right[...]

    def face_copy(sweep, f):
        if f < 2:
            to = (i + (1 if f == 1 else -1), j, k)
        else:
            to = (i, j + (1 if f == 3 else -1), k)
        return pltpu.make_async_remote_copy(
            solved.at[sweep, pl.ds(f * face, face)],
            face_in.at[sweep, f ^ 1],
            face_sem.at[sweep, f, 0],
            face_sem.at[sweep, f ^ 1, 1],
            device_id=to,
            device_id_type=MESH,
        )

    def await_face(sweep, f):
        to = ((i - 1, j, k), (i + 1, j, k), (i, j - 1, k), (i, j + 1, k))[f]
        pltpu.make_async_remote_copy(
            solved.at[sweep, pl.ds((f ^ 1) * face, face)],
            face_in.at[sweep, f],
            face_sem.at[sweep, f ^ 1, 0],
            face_sem.at[sweep, f, 1],
            device_id=to,
            device_id_type=MESH,
        ).wait_recv()

    def has(f):
        return (i > 0, i < nx - 1, j > 0, j < ny - 1)[f]

    def send_face(sweep, f):
        @pl.when(has(f))
        def _():
            face_copy(sweep, f).start()

    def pack(sweep, coefficient):
        terms = coefficient[group * limit : group * limit + count]
        terms = jnp.concatenate([terms[:, :half], terms[:, half:]], axis=0).astype(BF16)
        for t in range(group):
            own = coefficient[t * limit : (t + 1) * limit].astype(BF16)
            tx[sweep, t, 0:limit, :] = own[:, :half]
            tx[sweep, t, limit : 2 * limit, :] = own[:, half:]
            tx[sweep, t, 2 * limit :, :] = terms

        def send_group(step):
            a, c = member(step)
            pltpu.make_async_remote_copy(
                tx.at[sweep, a * nz + c],
                rx.at[sweep, me],
                group_sem.at[sweep, 0],
                group_sem.at[sweep, 1],
                device_id=(a, j, c),
                device_id_type=MESH,
            ).start()

        each(group - 1, send_group)
        rx[sweep, me] = tx[sweep, me]

    def forward(sweep):
        everyone = pltpu.make_async_remote_copy(
            tx.at[sweep, pl.ds(0, group - 1)],
            rx.at[sweep, pl.ds(0, group - 1)],
            group_sem.at[sweep, 0],
            group_sem.at[sweep, 1],
            device_id=(i, in_line(0), k),
            device_id_type=MESH,
        )
        everyone.wait_recv()
        for s in range(group):
            gathered[sweep, j, pl.ds(s * twice, twice), :] = rx[sweep, s, 2 * limit :, :]

        def send_line(step):
            pltpu.make_async_remote_copy(
                gathered.at[sweep, j],
                gathered.at[sweep, j],
                line_sem.at[sweep, 0],
                line_sem.at[sweep, 1],
                device_id=(i, in_line(step), k),
                device_id_type=MESH,
            ).start()

        each(ny - 1, send_line)
        arrived = rx[sweep, 0, 0 : 2 * limit, :].astype(F32)
        for s in range(1, group):
            arrived = arrived + rx[sweep, s, 0 : 2 * limit, :].astype(F32)
        joint[0:limit, :] = jnp.concatenate(
            [arrived[:limit], arrived[limit:]], axis=1
        ).astype(BF16)

    for sweep in range(ITERS):
        if sweep > 0:
            pack(sweep, jnp.dot(early[...], rounded[...], preferred_element_type=F32))
        for f in range(6):
            if sweep == 0:
                load_rows[f].wait()
            part = pl.ds(f * face, face)
            product = jnp.dot(
                inverse[part, :], rounded[...], preferred_element_type=F32
            ).astype(BF16)
            solved[sweep, part, :] = product
            if f < 4:
                send_face(sweep, f)
            if f == 4 and sweep > 0:
                forward(sweep)

        if sweep == 0:
            pack(sweep, jnp.dot(stacked[...], solved[sweep], preferred_element_type=F32))
            others = names.at[pl.ds(0, group - 1)]
            pltpu.make_async_remote_copy(
                others, others, name_sem.at[0], name_sem.at[1],
                device_id=(i, in_line(0), k), device_id_type=MESH,
            ).wait()
            every_name[j] = jnp.sum(names[...], axis=0)

            def send_line_names(step):
                pltpu.make_async_remote_copy(
                    every_name.at[j], every_name.at[j], name_sem.at[2], name_sem.at[3],
                    device_id=(i, in_line(step), k), device_id_type=MESH,
                ).start()

            each(ny - 1, send_line_names)

        for f in range(6):
            part = pl.ds(f * face, face)
            value = solved[sweep, part, :].astype(F32)
            source = right[part, :].astype(F32)
            before = source if sweep == 0 else final[part, :]
            base[part, :] = before + source - value

        if sweep == 0:
            forward(sweep)

        if sweep == 0:
            lines = coarse.at[pl.ds(0, ny - 1)]
            pltpu.make_async_remote_copy(
                lines, lines, coarse_sem.at[0], coarse_sem.at[1],
                device_id=(i, in_line(0), k), device_id_type=MESH,
            ).wait()
            lines = every_name.at[pl.ds(0, ny - 1)]
            pltpu.make_async_remote_copy(
                lines, lines, name_sem.at[2], name_sem.at[3],
                device_id=(i, in_line(0), k), device_id_type=MESH,
            ).wait()
            for n in range(6):
                part = pl.ds(n * face, face)
                early[:, part] = jnp.dot(
                    stacked[...], inverse[:, part], preferred_element_type=F32
                ).astype(BF16)
            row = lax.broadcasted_iota(jnp.int32, (twice, width), 0)
            lane = lax.broadcasted_iota(jnp.int32, (twice, width), 1)
            ids = jnp.zeros((twice, width), jnp.int32)
            for q in range(count):
                ids = jnp.where(lax.rem(row, count) == q, corner[q], ids)
            numbers = lax.broadcasted_iota(jnp.int32, (count, width), 1).astype(F32)
            picks = jnp.where(ids == lane, 1.0, 0.0).astype(BF16)
            depth = width // ny
            chosen = jnp.zeros((twice, width), F32)
            for y in range(ny):
                chosen = chosen + jnp.dot(
                    picks[:, y * depth : (y + 1) * depth], coarse[y], preferred_element_type=F32
                )
            chosen = chosen.astype(BF16)
            span = group * twice
            upper = lax.broadcasted_iota(jnp.int32, (twice, span), 0) // count
            lower = lax.rem(lax.broadcasted_iota(jnp.int32, (twice, span), 1), twice) // count
            for y in range(ny):
                named_y = every_name[y]
                for s in range(group):
                    one = jnp.where(named_y[:, s : s + 1] == numbers, 1.0, 0.0)
                    hot[pl.ds(s * twice, twice), :] = jnp.concatenate(
                        [one, one], axis=0
                    ).astype(BF16)
                entries_y = lax.dot_general(
                    chosen, hot[...], (((1,), (1,)), ((), ())), preferred_element_type=F32
                )
                mixing[y] = jnp.where(upper == lower, entries_y, 0.0).astype(BF16)

        pltpu.make_async_remote_copy(
            gathered.at[sweep, pl.ds(0, ny - 1)],
            gathered.at[sweep, pl.ds(0, ny - 1)],
            line_sem.at[sweep, 0],
            line_sem.at[sweep, 1],
            device_id=(i, in_line(0), k),
            device_id_type=MESH,
        ).wait_recv()
        picked = jnp.zeros((twice, half), F32)
        for y in range(ny):
            picked = picked + jnp.dot(mixing[y], gathered[sweep, y], preferred_element_type=F32)
        picked = jnp.concatenate([picked[:count], picked[count:]], axis=1)
        joint[limit:, :] = jnp.concatenate(
            [picked, jnp.zeros((twice - count, columns), F32)], axis=0
        ).astype(BF16)

        for f in (4, 5, 2, 3, 0, 1):
            part = pl.ds(f * face, face)
            if f < 4:

                @pl.when(has(f))
                def _():
                    await_face(sweep, f)

            value = base[part, :] - jnp.dot(
                lifted[part, :], joint[...], preferred_element_type=F32
            )
            if f < 4:
                value = value + link[f].astype(F32) * face_in[sweep, f].astype(F32)
            final[part, :] = value
            rounded[part, :] = value.astype(BF16)
            if sweep == ITERS - 1:
                pltpu.make_async_copy(
                    final.at[part], out_hbm.at[part], store_sem.at[f]
                ).start()

    for f in range(6):
        part = pl.ds(f * face, face)
        field[part, :] = jnp.dot(
            inverse[part, :], rounded[...], preferred_element_type=F32
        ).astype(BF16)
        pltpu.make_async_copy(field.at[part], field_hbm.at[part], store_sem.at[6 + f]).start()

    for sweep in range(ITERS):
        for f in range(4):

            @pl.when(has(f))
            def _():
                face_copy(sweep, f).wait_send()

        pltpu.make_async_remote_copy(
            tx.at[sweep, pl.ds(0, group - 1)],
            rx.at[sweep, pl.ds(0, group - 1)],
            group_sem.at[sweep, 0],
            group_sem.at[sweep, 1],
            device_id=(i, in_line(0), k),
            device_id_type=MESH,
        ).wait_send()
        pltpu.make_async_remote_copy(
            gathered.at[sweep, pl.ds(0, ny - 1)],
            gathered.at[sweep, pl.ds(0, ny - 1)],
            line_sem.at[sweep, 0],
            line_sem.at[sweep, 1],
            device_id=(i, in_line(0), k),
            device_id_type=MESH,
        ).wait_send()
    for f in range(6):
        part = pl.ds(f * face, face)
        pltpu.make_async_copy(final.at[part], out_hbm.at[part], store_sem.at[f]).wait()
        pltpu.make_async_copy(field.at[part], field_hbm.at[part], store_sem.at[6 + f]).wait()


def body(
    right_side,
    interface_inverse,
    face_link,
    far_target,
    far_rank,
    far_basis,
    patch_basis,
    corner_basis,
    corner_row,
    coarse_inverse,
):
    nx, ny, nz = (lax.axis_size(name) for name in ("sx", "sy", "sz"))
    group = nx * nz
    order = interface_inverse.shape[-1]
    columns = right_side.shape[-1]
    face = order // 6
    entries, limit = far_basis.shape[-3:-1]
    count = corner_row.shape[-1]
    depth, width = coarse_inverse.shape
    twice = 2 * count
    half = columns // 2
    stack = group * limit + twice
    message = 2 * limit + twice
    lanes = -(-group // 128) * 128
    smem = pl.BlockSpec(memory_space=pltpu.SMEM)
    hbm = pl.BlockSpec(memory_space=pl.ANY)
    scratch = [
        pltpu.VMEM((order, columns), BF16),
        pltpu.VMEM((order, order), BF16),
        pltpu.VMEM((entries * limit, order), BF16),
        pltpu.VMEM((limit, order), BF16),
        pltpu.VMEM((count, order), BF16),
        pltpu.VMEM((ny, depth, width), BF16),
        pltpu.VMEM((stack, order), BF16),
        pltpu.VMEM((stack, order), BF16),
        pltpu.VMEM((order, limit + twice), BF16),
        pltpu.VMEM((group, count, lanes), F32),
        pltpu.VMEM((ny, count, lanes), F32),
        pltpu.VMEM((group * twice, width), BF16),
        pltpu.VMEM((ny, twice, group * twice), BF16),
        pltpu.VMEM((order, columns), BF16),
        pltpu.VMEM((ITERS, order, columns), BF16),
        pltpu.VMEM((order, columns), F32),
        pltpu.VMEM((ITERS, 4, face, columns), BF16),
        pltpu.VMEM((ITERS, group, message, half), BF16),
        pltpu.VMEM((ITERS, group, message, half), BF16),
        pltpu.VMEM((ITERS, ny, group * twice, half), BF16),
        pltpu.VMEM((limit + twice, columns), BF16),
        pltpu.VMEM((order, columns), F32),
        pltpu.VMEM((order, columns), BF16),
        pltpu.SemaphoreType.DMA((11,)),
        pltpu.SemaphoreType.DMA((12,)),
        pltpu.SemaphoreType.DMA((4,)),
        pltpu.SemaphoreType.DMA((2,)),
        pltpu.SemaphoreType.DMA((ITERS, 4, 2)),
        pltpu.SemaphoreType.DMA((ITERS, 2)),
        pltpu.SemaphoreType.DMA((ITERS, 2)),
    ]
    results = (
        jax.ShapeDtypeStruct((order, columns), F32),
        jax.ShapeDtypeStruct((order, columns), BF16),
    )
    multipliers, field = pl.pallas_call(
        functools.partial(kernel, (nx, ny, nz)),
        out_shape=results,
        in_specs=[smem] * 4 + [hbm] * 6,
        out_specs=(hbm, hbm),
        scratch_shapes=scratch,
        compiler_params=pltpu.CompilerParams(
            collective_id=0, has_side_effects=True, vmem_limit_bytes=60 * 1024 * 1024
        ),
    )(
        face_link.reshape(-1),
        far_target.reshape(-1),
        far_rank.reshape(-1),
        corner_row.reshape(-1),
        right_side.reshape(order, columns),
        interface_inverse.reshape(order, order),
        far_basis.reshape(entries * limit, order),
        patch_basis.reshape(limit, order),
        corner_basis.reshape(count, order),
        coarse_inverse,
    )
    return multipliers.reshape(right_side.shape), field.reshape(right_side.shape)


def solution(mesh):
    wide = P("sx", "sy", "sz", None, None)
    return jax.shard_map(
        body,
        mesh=mesh,
        in_specs=(
            wide,
            wide,
            P("sx", "sy", "sz", None),
            wide,
            P("sx", "sy", "sz", None),
            P("sx", "sy", "sz", None, None, None),
            wide,
            wide,
            P("sx", "sy", "sz", None),
            P("sy", None),
        ),
        out_specs=(wide, wide),
        check_vma=False,
    )
```
